32 devices in a mesh: groups: 2 (over x), loop: 8 (over z, y), narrow: 2 (over core).
Axes of the slice: x: 2, y: 2, z: 4, core: 2. Of those that a mesh axis runs over, the one named last changes fastest.
Arguments:
- src_points: bfloat16 [512, 64, 128], P(('groups', 'loop', 'narrow')), parts along dimension 0
- tgt_points: bfloat16 [128, 64, 128], P(('groups', 'loop')), parts along dimension 0
- block_list: int32 [512, 24], P(('groups', 'loop', 'narrow')), parts along dimension 0, may hold values from 0 to 63, as said below
- list_len: int32 [512], P(('groups', 'loop', 'narrow')), parts along dimension 0, may hold values from 1 to 24
- src_counts: int32 [512], P(('groups', 'loop', 'narrow')), parts along dimension 0, may hold values from 1 to 128
- tgt_counts: int32 [128], P(('groups', 'loop')), parts along dimension 0, may hold values from 1 to 128
Outputs:
- src_field: float32 [512, 128], P(('groups', 'loop', 'narrow')), parts along dimension 0
- tgt_field: float32 [128, 128], P(('groups', 'loop')), parts along dimension 0
The draws below stay inside these ranges and needn't reach their ends.
There are 2 independent parts, one for each index of `groups`. The reference program is written for one: setup_inputs(seed, part) draws one part's arguments, and reference() takes and returns one part's arrays. A program takes and returns all parts, laid end to end along the dimension named above; each array names one. Nothing has to cross between parts.
Inputs may be any that keep to these rules, and one draw needn't show every extreme that they name: `block_list`: every entry of row i names a target block whose loop position t // 8 lies within 3 positions, cyclically over the loop's 8 positions, of the source block's loop position i // 32; only the first list_len[i] entries are used; every target block is named by a used entry of some source block.
All inputs are finite; a program needn't handle non-finite values.
Results may differ from the reference program's by a relative error of at most 0.0003.
Values may be sent and summed in bfloat16 or wider, within the bound.
A program may use at most 64 MiB of HBM per device.

```python
import jax
import jax.numpy as jnp
from jax import lax

FEAT = 64
BLOCK = 128
SB_DEV = 16
TB_DEV = 8
SLOTS = 24
REACH = 3
ITERS = 2
NS = 256
NT = 64
N_LOOP = 8
N_NARROW = 2


def cluster_cells(key, blocks):
    center_key, cell_key = jax.random.split(key, 2)
    center = 0.25 * jax.random.normal(center_key, (blocks, FEAT, 1), jnp.float32)
    cells = center + 0.2 * jax.random.normal(cell_key, (blocks, FEAT, BLOCK), jnp.float32)
    return cells.astype(jnp.bfloat16)


def slot_lengths(key):
    key = jax.random.fold_in(key, 41)
    first_key, spot_key = jax.random.split(key)
    lengths = jax.random.randint(first_key, (NS,), 1, SLOTS + 1)
    spot = jax.random.randint(spot_key, (), 0, NS)
    return lengths.at[spot].set(SLOTS).astype(jnp.int32)


def filled_counts(key, blocks):
    first_key, spot_key = jax.random.split(key)
    counts = jax.random.randint(first_key, (blocks,), 1, BLOCK + 1)
    spot = jax.random.randint(spot_key, (), 0, blocks)
    return counts.at[spot].set(BLOCK).astype(jnp.int32)


def draw_src_points(key, part):
    key = jax.random.fold_in(key, 1)
    return cluster_cells(key, NS)


def draw_tgt_points(key, part):
    key = jax.random.fold_in(key, 2)
    return cluster_cells(key, NT)


def draw_list_len(key, part):
    return slot_lengths(key)


def draw_block_list(key, part):
    lengths = slot_lengths(key)
    key = jax.random.fold_in(key, 5)
    offset_key, within_key, place_key = jax.random.split(key, 3)
    rows = jnp.arange(NS)
    position = rows // (SB_DEV * N_NARROW)
    local_row = rows % (SB_DEV * N_NARROW)
    offsets = jax.random.randint(offset_key, (NS, SLOTS), -REACH, REACH + 1)
    within = jax.random.randint(within_key, (NS, SLOTS), 0, TB_DEV)
    homes = jnp.mod(position[:, None] + offsets, N_LOOP)
    listed = homes * TB_DEV + within
    cover = position * TB_DEV + local_row % TB_DEV
    place = jax.random.randint(place_key, (NS,), 0, lengths)
    listed = jnp.where(jnp.arange(SLOTS)[None, :] == place[:, None], cover[:, None], listed)
    return listed.astype(jnp.int32)


def draw_src_counts(key, part):
    key = jax.random.fold_in(key, 7)
    return filled_counts(key, NS)


def draw_tgt_counts(key, part):
    key = jax.random.fold_in(key, 8)
    return filled_counts(key, NT)


def setup_inputs(seed: int = 0, part: int = 0) -> dict:
    arg_keys = jax.random.split(jax.random.key(seed), 7)
    part_keys = jax.random.split(jax.random.fold_in(arg_keys[6], part), 7)
    src_points = draw_src_points(jax.random.fold_in(jax.random.fold_in(arg_keys[6], part), 71), part)
    tgt_points = draw_tgt_points(jax.random.fold_in(jax.random.fold_in(arg_keys[6], part), 71), part)
    block_list = draw_block_list(jax.random.fold_in(jax.random.fold_in(arg_keys[6], part), 71), part)
    list_len = draw_list_len(jax.random.fold_in(jax.random.fold_in(arg_keys[6], part), 71), part)
    src_counts = draw_src_counts(jax.random.fold_in(jax.random.fold_in(arg_keys[6], part), 71), part)
    tgt_counts = draw_tgt_counts(jax.random.fold_in(jax.random.fold_in(arg_keys[6], part), 71), part)
    return dict(src_points=src_points, tgt_points=tgt_points, block_list=block_list, list_len=list_len, src_counts=src_counts, tgt_counts=tgt_counts)


EPSILON = 0.05
FILL_VALUE = -1e30


def block_cost(source, source_sq, targets, target_sq):
    cross = jnp.einsum("dr,kdc->krc", source.astype(jnp.float32), targets.astype(jnp.float32), precision=lax.Precision.HIGHEST)
    return source_sq[None, :, None] + target_sq[:, None, :] - 2.0 * cross


def reference(src_points, tgt_points, block_list, list_len, src_counts, tgt_counts):
    row_iota = jnp.arange(BLOCK)
    src_valid = row_iota[None, :] < src_counts[:, None]
    tgt_valid = row_iota[None, :] < tgt_counts[:, None]
    slot_live = jnp.arange(SLOTS)[None, :] < list_len[:, None]
    src_squares = jnp.sum(jnp.square(src_points.astype(jnp.float32)), axis=1)
    tgt_squares = jnp.sum(jnp.square(tgt_points.astype(jnp.float32)), axis=1)
    tgt_field = jnp.zeros((NT, BLOCK), jnp.float32)
    src_field = jnp.zeros((NS, BLOCK), jnp.float32)
    flat_index = block_list.reshape(-1)
    for iteration in range(ITERS):
        masked = jnp.where(tgt_valid, tgt_field, FILL_VALUE)

        def row_block(inputs):
            source, source_sq, listed, slot_ok, row_ok = inputs
            pair_cost = block_cost(source, source_sq, tgt_points[listed], tgt_squares[listed])
            potential = masked[listed]
            allowed = slot_ok[:, None, None] & tgt_valid[listed][:, None, :]
            scores = jnp.where(allowed, (potential[:, None, :] - pair_cost) / EPSILON, FILL_VALUE)
            row_peak = jnp.max(scores, axis=(0, 2))
            summed = jnp.sum(jnp.where(allowed, jnp.exp(scores - row_peak[None, :, None]), 0.0), axis=(0, 2))
            return jnp.where(row_ok, -EPSILON * (row_peak + jnp.log(summed)), 0.0)

        src_field = lax.map(row_block, (src_points, src_squares, block_list, slot_live, src_valid))

        def column_block(inputs):
            source, source_sq, listed, slot_ok, row_field, row_ok = inputs
            pair_cost = block_cost(source, source_sq, tgt_points[listed], tgt_squares[listed])
            allowed = row_ok[None, :, None]
            scores = jnp.where(allowed, (row_field[None, :, None] - pair_cost) / EPSILON, FILL_VALUE)
            col_peak = jnp.max(scores, axis=1)
            summed = jnp.sum(jnp.where(allowed, jnp.exp(scores - col_peak[:, None, :]), 0.0), axis=1)
            return jnp.where(slot_ok[:, None], col_peak + jnp.log(summed), FILL_VALUE)

        partial_value = lax.map(column_block, (src_points, src_squares, block_list, slot_live, src_field, src_valid))
        partial_value = partial_value.reshape(NS * SLOTS, BLOCK)
        peak_value = jax.ops.segment_max(partial_value, flat_index, num_segments=NT)
        summed_all = jax.ops.segment_sum(jnp.exp(partial_value - peak_value[flat_index]), flat_index, num_segments=NT)
        tgt_field = jnp.where(tgt_valid, -EPSILON * (peak_value + jnp.log(summed_all)), 0.0)
    return src_field, tgt_field
```

```python
import functools
import math

import jax
import jax.numpy as jnp
from jax import lax
from jax.experimental import pallas as pl
from jax.experimental.pallas import tpu as pltpu
from jax.sharding import PartitionSpec as P

REACH = 3
ITERS = 2
EPSILON = 0.05
SCALE = math.log2(math.e) / EPSILON
DEAD = -1e30
EMPTY = -1e38
UNROLL = 4
STEP = 32


def half_step_kernel(
    final, idx_ref, len_ref, cnt_ref, src_ref, pts_ref, pot_ref, *refs
):
    if final:
        fld_ref, out_ref, add_ref, sco_ref, peak_ref, sum_ref = refs
    else:
        fld_ref = None
        out_ref, add_ref, sco_ref, peak_ref, sum_ref = refs
    blocks, feat, cells = src_ref.shape
    targets = pot_ref.shape[0]
    f32, bf16 = jnp.float32, jnp.bfloat16

    rows16 = lax.broadcasted_iota(jnp.int32, (16, cells), 0)

    def spread(t, carry):
        pot = pot_ref[pl.ds(t, 1), :]
        hi = pot.astype(bf16).astype(f32)
        rest = pot - hi
        mid = rest.astype(bf16).astype(f32)
        low = rest - mid
        tile = jnp.where(rows16 == 0, hi, jnp.where(rows16 == 1, mid, jnp.where(rows16 == 2, low, 0.0)))
        add_ref[t] = tile.astype(bf16)
        return carry

    lax.fori_loop(0, targets, spread, 0, unroll=8)
    add_ref[targets] = jnp.where(rows16 == 0, DEAD, 0.0).astype(bf16)
    peak_ref[...] = jnp.full(peak_ref.shape, EMPTY, f32)
    sum_ref[...] = jnp.zeros(sum_ref.shape, f32)

    def source_block(i, rows):
        length = len_ref[i]
        count = cnt_ref[i]
        groups = (length + (UNROLL - 1)) // UNROLL
        source = src_ref[i].astype(f32)
        scaled = source * (2.0 * SCALE)
        hi = scaled.astype(bf16).astype(f32)
        low = scaled - hi
        both = jnp.concatenate([hi, low], axis=0).T.astype(bf16)[:rows]
        ones = (lax.broadcasted_iota(jnp.int32, (rows, 16), 1) < 3).astype(f32).astype(bf16)
        left = jnp.concatenate([both, ones], axis=1)

        def pick(k):
            live = k < length
            t = idx_ref[i, jnp.minimum(k, length - 1)]
            return t, jnp.where(live, t, targets)

        def score_group(g, peak):
            for u in range(UNROLL):
                k = g * UNROLL + u
                t, ta = pick(k)
                right = jnp.concatenate([pts_ref[t], pts_ref[t], add_ref[ta]], axis=0)
                score = jnp.dot(left, right, preferred_element_type=f32)
                sco_ref[k, :rows, :] = score
                peak = jnp.maximum(peak, score)
            return peak

        peak = lax.fori_loop(0, groups, score_group, jnp.full((rows, cells), EMPTY, f32))
        top = jnp.max(peak, axis=1, keepdims=True)

        def row_group(g, total):
            for u in range(UNROLL):
                total += jnp.exp2(sco_ref[g * UNROLL + u, :rows, :] - top)
            return total

        total = lax.fori_loop(0, groups, row_group, jnp.zeros((rows, cells), f32))
        row_lse = top + jnp.log2(jnp.sum(total, axis=1, keepdims=True))
        row_iota = lax.broadcasted_iota(jnp.int32, (rows, 1), 0)
        shift = jnp.where(row_iota < count, -row_lse, DEAD)

        if final:
            diag = lax.broadcasted_iota(jnp.int32, (rows, cells), 0) == lax.broadcasted_iota(
                jnp.int32, (rows, cells), 1
            )
            flat = jnp.sum(jnp.where(diag, row_lse, 0.0), axis=0, keepdims=True)
            squares = jnp.sum(source * source, axis=0, keepdims=True)
            lane = lax.broadcasted_iota(jnp.int32, (1, cells), 1)
            fld_ref[pl.ds(i, 1), :] = jnp.where(lane < count, squares - flat * (1.0 / SCALE), 0.0)

        def column_group(g, carry):
            for u in range(UNROLL):
                k = g * UNROLL + u
                _, ta = pick(k)
                shifted = (sco_ref[k, :rows, :] + shift).reshape(rows // 8, 8, cells)
                top8 = jnp.max(shifted, axis=0)
                sum8 = jnp.sum(jnp.exp2(shifted - top8[None]), axis=0)
                old = peak_ref[ta]
                new = jnp.maximum(old, top8)
                peak_ref[ta] = new
                sum_ref[ta] = sum_ref[ta] * jnp.exp2(old - new) + sum8 * jnp.exp2(top8 - new)
            return carry

        lax.fori_loop(0, groups, column_group, 0)

    def each_block(i, carry):
        steps = (cnt_ref[i] + (STEP - 1)) // STEP
        for s in range(1, cells // STEP + 1):

            @pl.when(steps == s)
            def _():
                source_block(i, s * STEP)

        return carry

    lax.fori_loop(0, blocks, each_block, 0)

    peak = peak_ref[:targets]
    top = jnp.max(peak, axis=1, keepdims=True)
    total = jnp.sum(sum_ref[:targets] * jnp.exp2(peak - top), axis=1)
    out_ref[...] = jnp.maximum(top[:, 0, :] + jnp.log2(total), EMPTY)


def half_step(final, block_list, list_len, src_counts, src_points, pts, pot):
    blocks, feat, cells = src_points.shape
    targets = pot.shape[0]
    slots = -(-block_list.shape[1] // UNROLL) * UNROLL
    smem = pl.BlockSpec(memory_space=pltpu.SMEM)
    vmem = pl.BlockSpec(memory_space=pltpu.VMEM)
    outs = [jax.ShapeDtypeStruct((targets, cells), jnp.float32)]
    if final:
        outs = [jax.ShapeDtypeStruct((blocks, cells), jnp.float32)] + outs
    return pl.pallas_call(
        functools.partial(half_step_kernel, final),
        out_shape=outs,
        in_specs=[smem, smem, smem, vmem, vmem, vmem],
        out_specs=[vmem] * len(outs),
        scratch_shapes=[
            pltpu.VMEM((targets + 1, 16, cells), jnp.bfloat16),
            pltpu.VMEM((slots, cells, cells), jnp.float32),
            pltpu.VMEM((targets + 1, 8, cells), jnp.float32),
            pltpu.VMEM((targets + 1, 8, cells), jnp.float32),
        ],
        compiler_params=pltpu.CompilerParams(vmem_limit_bytes=40 * 1024 * 1024),
    )(block_list, list_len, src_counts, src_points, pts, pot)


def local(src_points, tgt_points, block_list, list_len, src_counts, tgt_counts):
    loop_index = lax.axis_index("loop")
    tgt_blocks, _, cells = tgt_points.shape
    tgt_valid = jnp.arange(cells)[None, :] < tgt_counts[:, None]
    squares = jnp.sum(jnp.square(tgt_points.astype(jnp.float32)), axis=1)
    pot_home = jnp.where(tgt_valid, -SCALE * squares, DEAD)
    pts = lax.all_gather(tgt_points, "loop", tiled=True)
    pot = lax.all_gather(pot_home, "loop", tiled=True)
    for it in range(ITERS):
        final = it == ITERS - 1
        res = half_step(final, block_list, list_len, src_counts, src_points, pts, pot)
        every = lax.all_gather(res[-1], ("loop", "narrow"))
        top = jnp.max(every, axis=0)
        lse = top + jnp.log2(jnp.sum(jnp.exp2(every - top[None]), axis=0))
        pot = jnp.where(pot > 0.1 * DEAD, pot - lse, DEAD)
    mine = lax.dynamic_slice_in_dim(pot, loop_index * tgt_blocks, tgt_blocks, 0)
    tgt_field = jnp.where(tgt_valid, mine * (1.0 / SCALE) + squares, 0.0)
    return res[0], tgt_field


def solution(mesh):
    placed = (
        P(("groups", "loop", "narrow"), None, None),
        P(("groups", "loop"), None, None),
        P(("groups", "loop", "narrow"), None),
        P(("groups", "loop", "narrow")),
        P(("groups", "loop", "narrow")),
        P(("groups", "loop")),
    )
    return jax.shard_map(
        local,
        mesh=mesh,
        in_specs=placed,
        out_specs=(P(("groups", "loop", "narrow"), None), P(("groups", "loop"), None)),
        check_vma=False,
    )
```

```python
import functools
import math

import jax
import jax.numpy as jnp
from jax import lax
from jax.experimental import pallas as pl
from jax.experimental.pallas import tpu as pltpu
from jax.sharding import PartitionSpec as P

REACH = 3
ITERS = 2
EPSILON = 0.05
SCALE = math.log2(math.e) / EPSILON
DEAD = -1e30
EMPTY = -1e38
UNROLL = 4
STEP = 32


def half_step_kernel(
    final, idx_ref, len_ref, cnt_ref, src_ref, pts_ref, pot_ref, *refs
):
    if final:
        fld_ref, out_ref, add_ref, sco_ref, peak_ref, sum_ref = refs
    else:
        fld_ref = None
        out_ref, add_ref, sco_ref, peak_ref, sum_ref = refs
    blocks, feat, cells = src_ref.shape
    targets = pot_ref.shape[0]
    f32, bf16 = jnp.float32, jnp.bfloat16

    rows16 = lax.broadcasted_iota(jnp.int32, (16, cells), 0)

    def spread(t, carry):
        pot = pot_ref[pl.ds(t, 1), :]
        hi = pot.astype(bf16).astype(f32)
        rest = pot - hi
        mid = rest.astype(bf16).astype(f32)
        low = rest - mid
        tile = jnp.where(rows16 == 0, hi, jnp.where(rows16 == 1, mid, jnp.where(rows16 == 2, low, 0.0)))
        add_ref[t] = tile.astype(bf16)
        return carry

    lax.fori_loop(0, targets, spread, 0, unroll=8)
    add_ref[targets] = jnp.where(rows16 == 0, DEAD, 0.0).astype(bf16)
    peak_ref[...] = jnp.full(peak_ref.shape, EMPTY, f32)
    sum_ref[...] = jnp.zeros(sum_ref.shape, f32)

    def source_block(i, rows):
        length = len_ref[i]
        count = cnt_ref[i]
        groups = (length + (UNROLL - 1)) // UNROLL
        source = src_ref[i].astype(f32)
        scaled = source * (2.0 * SCALE)
        hi = scaled.astype(bf16).astype(f32)
        low = scaled - hi
        both = jnp.concatenate([hi, low], axis=0).T.astype(bf16)[:rows]
        ones = (lax.broadcasted_iota(jnp.int32, (rows, 16), 1) < 3).astype(f32).astype(bf16)
        left = jnp.concatenate([both, ones], axis=1)

        def pick(k):
            live = k < length
            t = idx_ref[i, jnp.minimum(k, length - 1)]
            return t, jnp.where(live, t, targets)

        def score_group(g, peak):
            for u in range(UNROLL):
                k = g * UNROLL + u
                t, ta = pick(k)
                right = jnp.concatenate([pts_ref[t], pts_ref[t], add_ref[ta]], axis=0)
                score = jnp.dot(left, right, preferred_element_type=f32)
                sco_ref[k, :rows, :] = score
                peak = jnp.maximum(peak, score)
            return peak

        peak = lax.fori_loop(0, groups, score_group, jnp.full((rows, cells), EMPTY, f32))
        top = jnp.max(peak, axis=1, keepdims=True)

        def row_group(g, total):
            for u in range(UNROLL):
                total += jnp.exp2(sco_ref[g * UNROLL + u, :rows, :] - top)
            return total

        total = lax.fori_loop(0, groups, row_group, jnp.zeros((rows, cells), f32))
        row_lse = top + jnp.log2(jnp.sum(total, axis=1, keepdims=True))
        row_iota = lax.broadcasted_iota(jnp.int32, (rows, 1), 0)
        shift = jnp.where(row_iota < count, -row_lse, DEAD)

        if final:
            diag = lax.broadcasted_iota(jnp.int32, (rows, cells), 0) == lax.broadcasted_iota(
                jnp.int32, (rows, cells), 1
            )
            flat = jnp.sum(jnp.where(diag, row_lse, 0.0), axis=0, keepdims=True)
            squares = jnp.sum(source * source, axis=0, keepdims=True)
            lane = lax.broadcasted_iota(jnp.int32, (1, cells), 1)
            fld_ref[pl.ds(i, 1), :] = jnp.where(lane < count, squares - flat * (1.0 / SCALE), 0.0)

        def column_group(g, carry):
            for u in range(UNROLL):
                k = g * UNROLL + u
                _, ta = pick(k)
                shifted = (sco_ref[k, :rows, :] + shift).reshape(rows // 8, 8, cells)
                top8 = jnp.max(shifted, axis=0)
                sum8 = jnp.sum(jnp.exp2(shifted - top8[None]), axis=0)
                old = peak_ref[ta]
                new = jnp.maximum(old, top8)
                peak_ref[ta] = new
                sum_ref[ta] = sum_ref[ta] * jnp.exp2(old - new) + sum8 * jnp.exp2(top8 - new)
            return carry

        lax.fori_loop(0, groups, column_group, 0)

    def each_block(i, carry):
        steps = (cnt_ref[i] + (STEP - 1)) // STEP
        for s in range(1, cells // STEP + 1):

            @pl.when(steps == s)
            def _():
                source_block(i, s * STEP)

        return carry

    lax.fori_loop(0, blocks, each_block, 0)

    peak = peak_ref[:targets]
    top = jnp.max(peak, axis=1, keepdims=True)
    total = jnp.sum(sum_ref[:targets] * jnp.exp2(peak - top), axis=1)
    out_ref[...] = jnp.maximum(top[:, 0, :] + jnp.log2(total), EMPTY)


def half_step(final, block_list, list_len, src_counts, src_points, pts, pot):
    blocks, feat, cells = src_points.shape
    targets = pot.shape[0]
    slots = -(-block_list.shape[1] // UNROLL) * UNROLL
    smem = pl.BlockSpec(memory_space=pltpu.SMEM)
    vmem = pl.BlockSpec(memory_space=pltpu.VMEM)
    outs = [jax.ShapeDtypeStruct((targets, cells), jnp.float32)]
    if final:
        outs = [jax.ShapeDtypeStruct((blocks, cells), jnp.float32)] + outs
    return pl.pallas_call(
        functools.partial(half_step_kernel, final),
        out_shape=outs,
        in_specs=[smem, smem, smem, vmem, vmem, vmem],
        out_specs=[vmem] * len(outs),
        scratch_shapes=[
            pltpu.VMEM((targets + 1, 16, cells), jnp.bfloat16),
            pltpu.VMEM((slots, cells, cells), jnp.float32),
            pltpu.VMEM((targets + 1, 8, cells), jnp.float32),
            pltpu.VMEM((targets + 1, 8, cells), jnp.float32),
        ],
        compiler_params=pltpu.CompilerParams(vmem_limit_bytes=40 * 1024 * 1024),
    )(block_list, list_len, src_counts, src_points, pts, pot)


MESH = pl.DeviceIdType.MESH
OFFSETS = tuple(d for d in range(-REACH, REACH + 1) if d != 0)


def place(distance):
    loop = lax.axis_size("loop")
    return lax.rem(lax.axis_index("loop") + (distance + loop), loop)


def greet(peers):
    barrier = pltpu.get_barrier_semaphore()
    for peer in peers:
        pl.semaphore_signal(barrier, inc=1, device_id=peer, device_id_type=MESH)
    pl.semaphore_wait(barrier, len(peers))


def remote(src, dst, send_sem, recv_sem, peer):
    return pltpu.make_async_remote_copy(
        src_ref=src, dst_ref=dst, send_sem=send_sem, recv_sem=recv_sem,
        device_id=peer, device_id_type=MESH,
    )


def gather_kernel(
    cnt_ref, tgt_ref, pts_ref, pot_ref,
    send_sem, recv_sem, pot_send, pot_recv, pass_send, pass_recv, own_sem,
):
    me, core = lax.axis_index("loop"), lax.axis_index("narrow")
    other = 1 - core
    blocks, feat, cells = tgt_ref.shape
    half = blocks // 2
    greet([{"loop": place(d), "narrow": core} for d in OFFSETS] + [{"loop": me, "narrow": other}])

    def part(home, which):
        return pts_ref.at[pl.ds(home * blocks + which * half, half)]

    sends = []
    for j, d in enumerate(OFFSETS):
        copy = remote(
            tgt_ref.at[pl.ds(core * half, half)], part(me, core),
            send_sem.at[j], recv_sem.at[j], {"loop": place(d), "narrow": core},
        )
        copy.start()
        sends.append(copy)
    own = pltpu.make_async_copy(tgt_ref, pts_ref.at[pl.ds(me * blocks, blocks)], own_sem)
    own.start()

    lane = lax.broadcasted_iota(jnp.int32, (1, cells), 1)
    rows = []
    for b in range(blocks):
        cell = tgt_ref[b].astype(jnp.float32)
        square = jnp.sum(cell * cell, axis=0, keepdims=True)
        rows.append(jnp.where(lane < cnt_ref[b], -SCALE * square, DEAD))
    mine = pot_ref.at[pl.ds(pl.multiple_of(me * blocks, 8), blocks)]
    mine[...] = jnp.concatenate(rows, axis=0)
    for j, d in enumerate(OFFSETS):
        copy = remote(mine, mine, pot_send.at[j], pot_recv.at[j], {"loop": place(d), "narrow": core})
        copy.start()
        sends.append(copy)

    partner = {"loop": me, "narrow": other}
    passed = []
    for j, d in enumerate(OFFSETS):
        got = part(place(-d), core)
        remote(got, got, send_sem.at[j], recv_sem.at[j], partner).wait_recv()
        copy = remote(got, got, pass_send.at[j], pass_recv.at[j], partner)
        copy.start()
        passed.append(copy)
    for j, d in enumerate(OFFSETS):
        home = place(-d)
        got = part(home, other)
        remote(got, got, pass_send.at[j], pass_recv.at[j], partner).wait_recv()
        got = pot_ref.at[pl.ds(pl.multiple_of(home * blocks, 8), blocks)]
        remote(got, got, pot_send.at[j], pot_recv.at[j], partner).wait_recv()
    for copy in sends + passed:
        copy.wait_send()
    own.wait()


def gather(tgt_counts, tgt_points):
    blocks, feat, cells = tgt_points.shape
    targets = blocks * lax.axis_size("loop")
    vmem = pl.BlockSpec(memory_space=pltpu.VMEM)
    dma = pltpu.SemaphoreType.DMA
    n = len(OFFSETS)
    return pl.pallas_call(
        gather_kernel,
        out_shape=[
            jax.ShapeDtypeStruct((targets, feat, cells), tgt_points.dtype),
            jax.ShapeDtypeStruct((targets, cells), jnp.float32),
        ],
        in_specs=[pl.BlockSpec(memory_space=pltpu.SMEM), vmem],
        out_specs=[vmem, vmem],
        scratch_shapes=[dma((n,))] * 6 + [dma],
        compiler_params=pltpu.CompilerParams(
            collective_id=0, has_side_effects=True, vmem_limit_bytes=24 * 1024 * 1024
        ),
    )(tgt_counts, tgt_points)


def exchange_kernel(
    last, cnt_ref, lse_ref, pot_ref, *refs
):
    if last:
        base_ref, out_ref, inbox, send_sem, recv_sem = refs
    else:
        out_ref, inbox, send_sem, recv_sem, pot_send, pot_recv = refs
    me, core = lax.axis_index("loop"), lax.axis_index("narrow")
    blocks = cnt_ref.shape[0]
    cells = lse_ref.shape[1]
    routes = [(d, side) for d in (0,) + OFFSETS for side in (0, 1) if (d, side) != (0, 0)]
    peers = [{"loop": place(d), "narrow": lax.rem(core + side, 2)} for d, side in routes]
    greet(peers)

    def rows(ref, home):
        return ref.at[pl.ds(pl.multiple_of(home * blocks, 8), blocks)]

    sends = []
    for j, (d, side) in enumerate(routes):
        copy = remote(rows(lse_ref, place(d)), inbox.at[j], send_sem.at[j], recv_sem.at[j], peers[j])
        copy.start()
        sends.append(copy)
    lane = lax.broadcasted_iota(jnp.int32, (1, cells), 1)
    lane = jnp.broadcast_to(lane, (blocks, cells))
    sub = lax.broadcasted_iota(jnp.int32, (blocks, cells), 0)
    live = lane < cnt_ref[0]
    for b in range(1, blocks):
        live = jnp.where(sub == b, (lane < cnt_ref[b]).astype(jnp.int32), live.astype(jnp.int32)) > 0
    for j in range(len(routes)):
        sends[j].wait_recv()
    top = own = rows(lse_ref, me)[...]
    for j in range(len(routes)):
        top = jnp.maximum(top, inbox[j])
    total = jnp.exp2(own - top)
    for j in range(len(routes)):
        total += jnp.exp2(inbox[j] - top)
    pot = rows(pot_ref, me)[...] - (top + jnp.log2(total))
    if last:
        out_ref[...] = jnp.where(live, (pot - rows(base_ref, me)[...]) * (1.0 / SCALE), 0.0)
    else:
        mine = rows(out_ref, me)
        mine[...] = jnp.where(live, pot, DEAD)
        for j, d in enumerate(OFFSETS):
            copy = remote(mine, mine, pot_send.at[j], pot_recv.at[j], {"loop": place(d), "narrow": core})
            copy.start()
            sends.append(copy)
        for j, d in enumerate(OFFSETS):
            got = rows(out_ref, place(-d))
            remote(got, got, pot_send.at[j], pot_recv.at[j], {"loop": me, "narrow": 1 - core}).wait_recv()
    for copy in sends:
        copy.wait_send()


def exchange(last, tgt_counts, lse, pot, *base):
    targets, cells = lse.shape
    blocks = tgt_counts.shape[0]
    vmem = pl.BlockSpec(memory_space=pltpu.VMEM)
    dma = pltpu.SemaphoreType.DMA
    n = 2 * len(OFFSETS) + 1
    return pl.pallas_call(
        functools.partial(exchange_kernel, last),
        out_shape=jax.ShapeDtypeStruct((blocks if last else targets, cells), jnp.float32),
        in_specs=[pl.BlockSpec(memory_space=pltpu.SMEM)] + [vmem] * (2 + len(base)),
        out_specs=vmem,
        scratch_shapes=[pltpu.VMEM((n, blocks, cells), jnp.float32), dma((n,)), dma((n,))]
        + ([] if last else [dma((len(OFFSETS),))] * 2),
        compiler_params=pltpu.CompilerParams(collective_id=2 if last else 1, has_side_effects=True),
    )(tgt_counts, lse, pot, *base)


def local(src_points, tgt_points, block_list, list_len, src_counts, tgt_counts):
    pts, first = gather(tgt_counts, tgt_points)
    listed = (block_list, list_len, src_counts, src_points, pts)
    (lse,) = half_step(False, *listed, first)
    pot = exchange(False, tgt_counts, lse, first)
    for it in range(1, ITERS - 1):
        (lse,) = half_step(False, *listed, pot)
        pot = exchange(False, tgt_counts, lse, pot)
    src_field, lse = half_step(True, *listed, pot)
    return src_field, exchange(True, tgt_counts, lse, pot, first)


def solution(mesh):
    placed = (
        P(("groups", "loop", "narrow"), None, None),
        P(("groups", "loop"), None, None),
        P(("groups", "loop", "narrow"), None),
        P(("groups", "loop", "narrow")),
        P(("groups", "loop", "narrow")),
        P(("groups", "loop")),
    )
    return jax.shard_map(
        local,
        mesh=mesh,
        in_specs=placed,
        out_specs=(P(("groups", "loop", "narrow"), None), P(("groups", "loop"), None)),
        check_vma=False,
    )
```

```python
import functools
import math

import jax
import jax.numpy as jnp
from jax import lax
from jax.experimental import pallas as pl
from jax.experimental.pallas import tpu as pltpu
from jax.sharding import PartitionSpec as P

REACH = 3
ITERS = 2
EPSILON = 0.05
SCALE = math.log2(math.e) / EPSILON
DEAD = -1e30
EMPTY = -1e38
WIDE = 8
NARROW = 4
STEP = 32


def half_step_kernel(
    final, idx_ref, len_ref, cnt_ref, src_ref, pts_ref, pot_ref, *refs
):
    if final:
        fld_ref, out_ref, add_ref, left_ref, sco_ref, top_ref, tot_ref, peak_ref, sum_ref = refs
    else:
        fld_ref = None
        out_ref, add_ref, left_ref, sco_ref, top_ref, tot_ref, peak_ref, sum_ref = refs
    blocks, feat, cells = src_ref.shape
    targets = pot_ref.shape[0]
    f32, bf16 = jnp.float32, jnp.bfloat16
    depth = feat + 16

    rows16 = lax.broadcasted_iota(jnp.int32, (16, cells), 0)

    def spread(t, carry):
        pot = pot_ref[pl.ds(t, 1), :] * (1.0 / SCALE)
        hi = pot.astype(bf16).astype(f32)
        rest = pot - hi
        mid = rest.astype(bf16).astype(f32)
        low = rest - mid
        tile = jnp.where(rows16 == 0, hi, jnp.where(rows16 == 1, mid, jnp.where(rows16 == 2, low, 0.0)))
        add_ref[t] = tile.astype(bf16)
        return carry

    lax.fori_loop(0, targets, spread, 0, unroll=8)
    add_ref[targets] = jnp.where(rows16 == 0, DEAD, 0.0).astype(bf16)
    peak_ref[...] = jnp.full(peak_ref.shape, EMPTY, f32)
    sum_ref[...] = jnp.zeros(sum_ref.shape, f32)

    ones = (lax.broadcasted_iota(jnp.int32, (cells - feat, cells), 0) < 3).astype(f32)

    def turn(i, carry):
        doubled = src_ref[i].astype(f32) * 2.0
        left_ref[i] = jnp.concatenate([doubled, ones], axis=0).T.astype(bf16)
        return carry

    lax.fori_loop(0, blocks, turn, 0, unroll=4)

    def pick(i, k):
        length = len_ref[i]
        t = idx_ref[i, jnp.minimum(k, length - 1)]
        return t, jnp.where(k < length, t, targets)

    def score_block(i, rows):
        left = left_ref[i, :rows, :depth]

        def group(g, carry):
            peak, total = carry
            scores = []
            for u in range(WIDE):
                k = g * WIDE + u
                t, ta = pick(i, k)
                right = jnp.concatenate([pts_ref[t], add_ref[ta]], axis=0)
                score = jnp.dot(left, right, preferred_element_type=f32) * SCALE
                sco_ref[i, k, :rows, :] = score
                scores.append(score)
            new = peak
            for score in scores:
                new = jnp.maximum(new, score)
            total = total * jnp.exp2(peak - new)
            for score in scores:
                total += jnp.exp2(score - new)
            return new, total

        groups = (len_ref[i] + (WIDE - 1)) // WIDE
        start = (jnp.full((rows, cells), EMPTY, f32), jnp.zeros((rows, cells), f32))
        peak, total = lax.fori_loop(0, groups, group, start)
        top_ref[i, :rows, :] = peak
        tot_ref[i, :rows, :] = total

    def close_rows(i, carry):
        count = cnt_ref[i]
        peak = top_ref[i]
        top = jnp.max(peak, axis=1, keepdims=True)
        total = jnp.sum(tot_ref[i] * jnp.exp2(peak - top), axis=1, keepdims=True)
        row_lse = jnp.broadcast_to(top + jnp.log2(total), (cells, cells))
        sub = lax.broadcasted_iota(jnp.int32, (cells, cells), 0)
        top_ref[i] = jnp.where(sub < count, -row_lse, DEAD)
        if final:
            source = src_ref[i].astype(f32)
            lane = lax.broadcasted_iota(jnp.int32, (cells, cells), 1)
            flat = jnp.sum(jnp.where(sub == lane, row_lse, 0.0), axis=0, keepdims=True)
            squares = jnp.sum(source * source, axis=0, keepdims=True)
            fld_ref[pl.ds(i, 1), :] = jnp.where(
                lane[:1] < count, squares - flat * (1.0 / SCALE), 0.0
            )
        return carry

    def column_block(i, rows):
        shift = top_ref[i, :rows, :]

        def group(g, carry):
            for u in range(NARROW):
                k = g * NARROW + u
                _, ta = pick(i, k)
                shifted = (sco_ref[i, k, :rows, :] + shift).reshape(rows // 8, 8, cells)
                top8 = jnp.max(shifted, axis=0)
                sum8 = jnp.sum(jnp.exp2(shifted - top8[None]), axis=0)
                old = peak_ref[ta]
                new = jnp.maximum(old, top8)
                peak_ref[ta] = new
                sum_ref[ta] = sum_ref[ta] * jnp.exp2(old - new) + sum8 * jnp.exp2(top8 - new)
            return carry

        lax.fori_loop(0, (len_ref[i] + (NARROW - 1)) // NARROW, group, 0)

    def over_blocks(work):
        def each(i, carry):
            steps = (cnt_ref[i] + (STEP - 1)) // STEP
            for s in range(1, cells // STEP + 1):
                pl.when(steps == s)(functools.partial(work, i, s * STEP))
            return carry

        lax.fori_loop(0, blocks, each, 0)

    over_blocks(score_block)
    lax.fori_loop(0, blocks, close_rows, 0, unroll=2)
    over_blocks(column_block)

    peak = peak_ref[:targets]
    top = jnp.max(peak, axis=1, keepdims=True)
    total = jnp.sum(sum_ref[:targets] * jnp.exp2(peak - top), axis=1)
    out_ref[...] = jnp.maximum(top[:, 0, :] + jnp.log2(total), EMPTY)


def half_step(final, block_list, list_len, src_counts, src_points, pts, pot):
    blocks, feat, cells = src_points.shape
    targets = pot.shape[0]
    slots = -(-block_list.shape[1] // WIDE) * WIDE
    smem = pl.BlockSpec(memory_space=pltpu.SMEM)
    vmem = pl.BlockSpec(memory_space=pltpu.VMEM)
    outs = [jax.ShapeDtypeStruct((targets, cells), jnp.float32)]
    if final:
        outs = [jax.ShapeDtypeStruct((blocks, cells), jnp.float32)] + outs
    return pl.pallas_call(
        functools.partial(half_step_kernel, final),
        out_shape=outs,
        in_specs=[smem, smem, smem, vmem, vmem, vmem],
        out_specs=[vmem] * len(outs),
        scratch_shapes=[
            pltpu.VMEM((targets + 1, 16, cells), jnp.bfloat16),
            pltpu.VMEM((blocks, cells, cells), jnp.bfloat16),
            pltpu.VMEM((blocks, slots, cells, cells), jnp.float32),
            pltpu.VMEM((blocks, cells, cells), jnp.float32),
            pltpu.VMEM((blocks, cells, cells), jnp.float32),
            pltpu.VMEM((targets + 1, 8, cells), jnp.float32),
            pltpu.VMEM((targets + 1, 8, cells), jnp.float32),
        ],
        compiler_params=pltpu.CompilerParams(vmem_limit_bytes=50 * 1024 * 1024),
    )(block_list, list_len, src_counts, src_points, pts, pot)


MESH = pl.DeviceIdType.MESH
OFFSETS = tuple(d for d in range(-REACH, REACH + 1) if d != 0)


def place(distance):
    loop = lax.axis_size("loop")
    return lax.rem(lax.axis_index("loop") + (distance + loop), loop)


def greet(peers):
    barrier = pltpu.get_barrier_semaphore()
    for peer in peers:
        pl.semaphore_signal(barrier, inc=1, device_id=peer, device_id_type=MESH)
    pl.semaphore_wait(barrier, len(peers))


def remote(src, dst, send_sem, recv_sem, peer):
    return pltpu.make_async_remote_copy(
        src_ref=src, dst_ref=dst, send_sem=send_sem, recv_sem=recv_sem,
        device_id=peer, device_id_type=MESH,
    )


def gather_kernel(
    cnt_ref, tgt_ref, pts_ref, pot_ref, live_ref,
    send_sem, recv_sem, pot_send, pot_recv, pass_send, pass_recv, own_sem,
):
    me, core = lax.axis_index("loop"), lax.axis_index("narrow")
    other = 1 - core
    blocks, feat, cells = tgt_ref.shape
    half = blocks // 2
    greet([{"loop": place(d), "narrow": core} for d in OFFSETS] + [{"loop": me, "narrow": other}])

    def part(home, which):
        return pts_ref.at[pl.ds(home * blocks + which * half, half)]

    sends = []
    for j, d in enumerate(OFFSETS):
        copy = remote(
            tgt_ref.at[pl.ds(core * half, half)], part(me, core),
            send_sem.at[j], recv_sem.at[j], {"loop": place(d), "narrow": core},
        )
        copy.start()
        sends.append(copy)
    own = pltpu.make_async_copy(tgt_ref, pts_ref.at[pl.ds(me * blocks, blocks)], own_sem)
    own.start()

    lane = lax.broadcasted_iota(jnp.int32, (1, cells), 1)
    rows, lives = [], []
    for b in range(blocks):
        cell = tgt_ref[b].astype(jnp.float32)
        square = jnp.sum(cell * cell, axis=0, keepdims=True)
        live = lane < cnt_ref[b]
        rows.append(jnp.where(live, -SCALE * square, DEAD))
        lives.append(jnp.where(live, 1.0, 0.0))
    live_ref[...] = jnp.concatenate(lives, axis=0)
    mine = pot_ref.at[pl.ds(pl.multiple_of(me * blocks, 8), blocks)]
    mine[...] = jnp.concatenate(rows, axis=0)
    for j, d in enumerate(OFFSETS):
        copy = remote(mine, mine, pot_send.at[j], pot_recv.at[j], {"loop": place(d), "narrow": core})
        copy.start()
        sends.append(copy)

    partner = {"loop": me, "narrow": other}
    passed = []
    for j, d in enumerate(OFFSETS):
        got = part(place(-d), core)
        remote(got, got, send_sem.at[j], recv_sem.at[j], partner).wait_recv()
        copy = remote(got, got, pass_send.at[j], pass_recv.at[j], partner)
        copy.start()
        passed.append(copy)
    for j, d in enumerate(OFFSETS):
        home = place(-d)
        got = part(home, other)
        remote(got, got, pass_send.at[j], pass_recv.at[j], partner).wait_recv()
        got = pot_ref.at[pl.ds(pl.multiple_of(home * blocks, 8), blocks)]
        remote(got, got, pot_send.at[j], pot_recv.at[j], partner).wait_recv()
    for copy in sends + passed:
        copy.wait_send()
    own.wait()


def gather(tgt_counts, tgt_points):
    blocks, feat, cells = tgt_points.shape
    targets = blocks * lax.axis_size("loop")
    vmem = pl.BlockSpec(memory_space=pltpu.VMEM)
    dma = pltpu.SemaphoreType.DMA
    n = len(OFFSETS)
    return pl.pallas_call(
        gather_kernel,
        out_shape=[
            jax.ShapeDtypeStruct((targets, feat, cells), tgt_points.dtype),
            jax.ShapeDtypeStruct((targets, cells), jnp.float32),
            jax.ShapeDtypeStruct((blocks, cells), jnp.float32),
        ],
        in_specs=[pl.BlockSpec(memory_space=pltpu.SMEM), vmem],
        out_specs=[vmem, vmem, vmem],
        scratch_shapes=[dma((n,))] * 6 + [dma],
        compiler_params=pltpu.CompilerParams(
            collective_id=0, has_side_effects=True, vmem_limit_bytes=24 * 1024 * 1024
        ),
    )(tgt_counts, tgt_points)


def exchange_kernel(
    last, live_ref, lse_ref, pot_ref, *refs
):
    if last:
        base_ref, out_ref, inbox, send_sem, recv_sem = refs
    else:
        out_ref, inbox, send_sem, recv_sem, pot_send, pot_recv = refs
    me, core = lax.axis_index("loop"), lax.axis_index("narrow")
    blocks = live_ref.shape[0]
    routes = [(d, side) for d in (0,) + OFFSETS for side in (0, 1) if (d, side) != (0, 0)]
    peers = [{"loop": place(d), "narrow": lax.rem(core + side, 2)} for d, side in routes]
    greet(peers)

    def rows(ref, home):
        return ref.at[pl.ds(pl.multiple_of(home * blocks, 8), blocks)]

    sends = []
    for j, (d, side) in enumerate(routes):
        copy = remote(rows(lse_ref, place(d)), inbox.at[j], send_sem.at[j], recv_sem.at[j], peers[j])
        copy.start()
        sends.append(copy)
    live = live_ref[...] > 0.5
    for j in range(len(routes)):
        sends[j].wait_recv()
    top = own = rows(lse_ref, me)[...]
    for j in range(len(routes)):
        top = jnp.maximum(top, inbox[j])
    total = jnp.exp2(own - top)
    for j in range(len(routes)):
        total += jnp.exp2(inbox[j] - top)
    pot = rows(pot_ref, me)[...] - (top + jnp.log2(total))
    if last:
        out_ref[...] = jnp.where(live, (pot - rows(base_ref, me)[...]) * (1.0 / SCALE), 0.0)
    else:
        mine = rows(out_ref, me)
        mine[...] = jnp.where(live, pot, DEAD)
        for j, d in enumerate(OFFSETS):
            copy = remote(mine, mine, pot_send.at[j], pot_recv.at[j], {"loop": place(d), "narrow": core})
            copy.start()
            sends.append(copy)
        for j, d in enumerate(OFFSETS):
            got = rows(out_ref, place(-d))
            remote(got, got, pot_send.at[j], pot_recv.at[j], {"loop": me, "narrow": 1 - core}).wait_recv()
    for copy in sends:
        copy.wait_send()


def exchange(last, alive, lse, pot, *base):
    targets, cells = lse.shape
    blocks = alive.shape[0]
    vmem = pl.BlockSpec(memory_space=pltpu.VMEM)
    dma = pltpu.SemaphoreType.DMA
    n = 2 * len(OFFSETS) + 1
    return pl.pallas_call(
        functools.partial(exchange_kernel, last),
        out_shape=jax.ShapeDtypeStruct((blocks if last else targets, cells), jnp.float32),
        in_specs=[vmem] * (3 + len(base)),
        out_specs=vmem,
        scratch_shapes=[pltpu.VMEM((n, blocks, cells), jnp.float32), dma((n,)), dma((n,))]
        + ([] if last else [dma((len(OFFSETS),))] * 2),
        compiler_params=pltpu.CompilerParams(collective_id=2 if last else 1, has_side_effects=True),
    )(alive, lse, pot, *base)


def local(src_points, tgt_points, block_list, list_len, src_counts, tgt_counts):
    pts, first, alive = gather(tgt_counts, tgt_points)
    listed = (block_list, list_len, src_counts, src_points, pts)
    (lse,) = half_step(False, *listed, first)
    pot = exchange(False, alive, lse, first)
    for it in range(1, ITERS - 1):
        (lse,) = half_step(False, *listed, pot)
        pot = exchange(False, alive, lse, pot)
    src_field, lse = half_step(True, *listed, pot)
    return src_field, exchange(True, alive, lse, pot, first)


def solution(mesh):
    placed = (
        P(("groups", "loop", "narrow"), None, None),
        P(("groups", "loop"), None, None),
        P(("groups", "loop", "narrow"), None),
        P(("groups", "loop", "narrow")),
        P(("groups", "loop", "narrow")),
        P(("groups", "loop")),
    )
    return jax.shard_map(
        local,
        mesh=mesh,
        in_specs=placed,
        out_specs=(P(("groups", "loop", "narrow"), None), P(("groups", "loop"), None)),
        check_vma=False,
    )
```
